1024 devices in a mesh: sx: 16 (over y_hi, x, core), sy: 4 (over y_lo), cr: 16 (over z).
Axes of the slice: x: 4, y: 8 (y_hi: 2, y_lo: 4; y = y_hi * 4 + y_lo), z: 16, core: 2. Of those that a mesh axis runs over, the one named last changes fastest.
Arguments:
- adjoint: float32 [256, 256, 512], P('cr', 'sx', 'sy'), may hold values from -6 to 6
- sensor_rows: bfloat16 [12288, 256, 512], P('cr', 'sx', 'sy'), may hold values from -0.015625 to 0.015625
- cell_ids: int32 [256, 512], P('sx', 'sy'), may hold values from 0 to 15
- mat_diag: float32 [16], replicated, may hold values from -0.15 to 0.15
- mat_cond: float32 [16], replicated, may hold values from 0.2 to 0.45
- cheb_coef: float32 [9], replicated, may hold values from 0.3 to 1
Outputs:
- smoothed: float32 [256, 256, 512], P('cr', 'sx', 'sy')
- panel: float32 [12288, 256], P('cr', ('sx', 'sy'))
The draws below stay inside these ranges and needn't reach their ends.
All inputs are finite; a program needn't handle non-finite values.
Results may differ from the reference program's by a relative error of at most 0.0029.
Values may be sent and summed in bfloat16 or wider, within the bound.
A program may use at most 32 MiB of HBM per device.

```python
import jax
import jax.numpy as jnp
from jax import lax

COLS = 256
DEG = 8
NMAT = 16
ROWS = 12288
NX = 256
NY = 512


def plant(drawn, own_key, least, largest):
    longest = drawn.shape.index(max(drawn.shape))
    spots = []
    for shift in (0, 1):
        where = [jax.random.randint(jax.random.fold_in(own_key, axis), (), 0, length) for axis, length in enumerate(drawn.shape)]
        where[longest] = (where[longest] + shift) % drawn.shape[longest]
        spots.append(tuple(where))
    return drawn.at[spots[0]].set(least).at[spots[1]].set(largest)


def levels(stream_key, extent, pieces, smallest, top_value):
    gain, own = 1.0, jax.random.fold_in(stream_key, 6)
    for position, shards_of in pieces:
        steps = jnp.exp(jax.random.uniform(jax.random.fold_in(own, position), (shards_of,), jnp.float32, smallest / len(pieces), top_value / len(pieces)))
        gain = gain * jnp.repeat(steps, extent[position] // shards_of).reshape([-1 if axis == position else 1 for axis in range(len(extent))])
    return gain


def gaussian(rng, dims, spread, reach, shards=(), held_as=jnp.bfloat16):
    drawn = jax.random.normal(rng, dims, jnp.float32) * spread
    if len(shards) > 0:
        drawn = levels(rng, dims, shards, -0.22, 0.18) * drawn
    return jnp.clip(drawn, min=-reach, max=reach).astype(held_as)


def setup_inputs(seed: int = 0) -> dict:
    seeds = jax.random.split(jax.random.key(seed), 7)
    return {
        "adjoint": gaussian(seeds[0], (COLS, NX, NY), 1.0, 6.0, ((0, 16), (1, 16), (2, 4)), jnp.float32),
        "sensor_rows": gaussian(seeds[1], (ROWS, NX, NY), (NX * NY) ** -0.5, 0.015625, ((0, 16), (1, 16), (2, 4))),
        "cell_ids": plant(jax.random.randint(seeds[2], (NX, NY), 0, NMAT), jax.random.fold_in(seeds[2], 1), 0, NMAT - 1).astype(jnp.int32),
        "mat_diag": jnp.clip(jax.random.uniform(seeds[3], (NMAT,), jnp.float32, -0.15, 0.15), -0.15, 0.15),
        "mat_cond": jnp.clip(jax.random.uniform(seeds[4], (NMAT,), jnp.float32, 0.2, 0.45), 0.2, 0.45),
        "cheb_coef": jnp.clip(jax.random.uniform(seeds[5], (DEG + 1,), jnp.float32, 0.3, 1.0), 0.3, 1.0),
    }


def apply_scaled(field, diag, cond):
    weighted = cond * field
    padded = jnp.pad(weighted, ((0, 0), (1, 1), (1, 1)))
    beside = padded[:, :-2, 1:-1] + padded[:, 2:, 1:-1]
    beside = beside + padded[:, 1:-1, :-2] + padded[:, 1:-1, 2:]
    return diag * field + cond * beside


def reference(adjoint, sensor_rows, cell_ids, mat_diag, mat_cond, cheb_coef):
    diag = mat_diag[cell_ids]
    cond = mat_cond[cell_ids]
    older = adjoint
    current = apply_scaled(adjoint, diag, cond)
    smoothed = cheb_coef[0] * adjoint + cheb_coef[1] * current
    for order in range(2, DEG + 1):
        newer = 2.0 * apply_scaled(current, diag, cond) - older
        older = current
        current = newer
        smoothed = smoothed + cheb_coef[order] * newer
    lowered = smoothed.astype(jnp.bfloat16)
    flat_rows = sensor_rows.reshape(sensor_rows.shape[0], -1)
    flat_cols = lowered.reshape(lowered.shape[0], -1)
    panel = lax.dot_general(flat_rows, flat_cols, (((1,), (1,)), ((), ())), preferred_element_type=jnp.float32)
    return smoothed, panel
```

```python
import functools

import jax
import jax.numpy as jnp
from jax import lax
from jax.experimental import pallas as pl
from jax.experimental.pallas import tpu as pltpu
from jax.sharding import PartitionSpec as P

DEG = 8
LANES = 128
HALF = LANES // 2
PIECES = 2
MESH = pl.DeviceIdType.MESH


def lane_iota(shape):
    return lax.broadcasted_iota(jnp.int32, shape, len(shape) - 1)


def roll(value, shift):
    return pltpu.roll(value, shift % LANES, value.ndim - 1)


def lookup(ids, table):
    out = jnp.zeros(ids.shape, jnp.float32)
    for material in range(table.shape[0]):
        out = jnp.where(ids == material, table[material], out)
    return out


def load_own(wide, scaled, main, acc, coef):
    nx = scaled.shape[1]
    for x in range(nx):
        for g in range(2):
            value = wide[pl.ds(g * 8 * nx + x, 8, stride=nx), :]
            if g == 1:
                value = roll(value, HALF)
            value = scaled[g, x] * value
            main[0, DEG + x, g] = value
            acc[x, g] = coef[0] * value


def pack_edges(main, packed, nx):
    lane = lane_iota((8, LANES))
    window = lax.rem(lane, HALF) // DEG
    low = lane < HALF
    for xb in range(nx // 8):
        first = jnp.zeros((8, LANES), jnp.float32)
        last = jnp.zeros((8, LANES), jnp.float32)
        for i in range(8):
            m0 = main[0, DEG + 8 * xb + i, 0]
            m1 = main[0, DEG + 8 * xb + i, 1]
            first = jnp.where(window == i, roll(jnp.where(low, m0, m1), 8 * i), first)
            last = jnp.where(window == i, roll(jnp.where(low, m1, m0), 8 * (i + 1)), last)
        packed[0, xb] = first
        packed[1, xb] = last


def unpack_edges(got, side):
    lane = lax.rem(lane_iota((8, LANES)), HALF)
    for xb in range(got.shape[1]):
        left = got[0, xb]
        right = got[1, xb]
        for i in range(8):
            value = jnp.where(lane >= HALF - DEG, roll(left, -8 * (i + 1)), 0.0)
            side[0, 8 * xb + i] = jnp.where(lane < DEG, roll(right, -8 * i), value)


def build_fields(ids, mat_diag, mat_cond, diag2, cond2):
    middle = ids[1]
    rows = middle.shape[0]
    lane = lane_iota((rows, LANES))
    in_half = lax.rem(lane, HALF)
    lower = lane < HALF
    left = jnp.where(lower, roll(ids[0], HALF), ids[0])
    right = jnp.where(lower, ids[2], roll(ids[2], HALF))
    edges = jnp.where(in_half < DEG, right, jnp.where(in_half >= HALF - DEG, left, -1))
    for t, tile in enumerate((middle, None, edges)):
        if tile is None:
            d, c = roll(diag, HALF), roll(cond, HALF)
        else:
            diag, cond = lookup(tile, mat_diag), lookup(tile, mat_cond)
            d, c = diag, cond
        diag2[t] = jnp.broadcast_to((2.0 * d)[:, None, :], (rows, 8, LANES))
        cond2[t] = jnp.broadcast_to((2.0 * c * c)[:, None, :], (rows, 8, LANES))


def own_cond(ids_ref, mat_cond, scaled, unscaled):
    cond = lookup(ids_ref[...], mat_cond)
    nx = cond.shape[0]
    for g in range(2):
        value = cond if g == 0 else roll(cond, HALF)
        scaled[g] = jnp.broadcast_to(value[:, None, :], (nx, 8, LANES))
        unscaled[g] = jnp.broadcast_to((1.0 / value)[:, None, :], (nx, 8, LANES))


def filter_steps(main, side, diag2, cond2, acc, coef, nx):
    rows = nx + 2 * DEG
    for k in range(1, DEG + 1):
        cur, new = (k + 1) % 2, k % 2
        cuts = [k] + [c for c in range(8, rows, 8) if k < c < rows - k] + [rows - k]
        for a, b in zip(cuts[:-1], cuts[1:]):
            lane = lane_iota((b - a, 8, LANES))
            whole = [main[cur, a - 1 : b + 1, 0], main[cur, a - 1 : b + 1, 1], side[cur, a - 1 : b + 1]]
            middle = [w[1:-1] for w in whole]
            before = [roll(m, 1) for m in middle]
            after = [roll(m, -1) for m in middle]
            wrap_b = (0, HALF)
            wrap_a = (LANES - 1, HALF - 1)
            for t in range(3 if k < DEG else 2):
                if t < 2:
                    lhs = jnp.where(lane == wrap_b[t], before[2], before[t])
                    rhs = jnp.where(lane == wrap_a[t], after[2], after[t])
                else:
                    lhs = jnp.where(lane == wrap_b[0], before[0], jnp.where(lane == wrap_b[1], before[1], before[2]))
                    rhs = jnp.where(lane == wrap_a[0], after[0], jnp.where(lane == wrap_a[1], after[1], after[2]))
                beside = (whole[t][:-2] + whole[t][2:]) + (lhs + rhs)
                value = diag2[t, a:b] * middle[t] + cond2[t, a:b] * beside
                if k == 1:
                    value = 0.5 * value
                elif t < 2:
                    value = value - main[new, a:b, t]
                else:
                    value = value - side[new, a:b]
                if t == 2:
                    side[new, a:b] = value
                else:
                    if k < DEG:
                        main[new, a:b, t] = value
                    if a >= DEG and b <= rows - DEG:
                        acc[a - DEG : b - DEG, t] = acc[a - DEG : b - DEG, t] + coef[k] * value


def finish(acc, unscaled, smooth, cols, nx):
    depth = cols.shape[-1]
    for x in range(nx):
        done = []
        for g in range(2):
            value = acc[x, g] * unscaled[g, x]
            if g == 1:
                value = roll(value, HALF)
            smooth[pl.ds(g * 8 * nx + x, 8, stride=nx), :] = value
            done.append(value)
        at = x * LANES
        cols[at // depth, 0, :, at % depth : at % depth + LANES] = jnp.concatenate(done, axis=0).astype(jnp.bfloat16)


def turn_rows(raw, flat):
    step = 16
    nx = raw.shape[1]

    def body(i, carry):
        at = pl.ds(pl.multiple_of(i * step, step), step)
        turned = jnp.swapaxes(raw[at], 0, 1)
        for x in range(nx):
            flat[at, x * LANES : (x + 1) * LANES] = turned[x]
        return carry

    lax.fori_loop(0, raw.shape[0] // step, body, 0)


def kernel(
    sizes,
    adj_hbm, rows_hbm, ids_ref, mat_diag, mat_cond, coef,
    smooth_hbm, panel_ref,
    wide, raw, flat, ids, scaled, unscaled, main, side, acc, packed, got, diag2, cond2, smooth, cols,
    out_a, in_a, out_b, in_b,
    local_sem, halo_send, halo_recv, z_send, z_recv, a_send, a_recv, b_send, b_recv,
):
    nsx, nsy, ncr = sizes
    low = nsx // 2
    me_x, me_y, me_z = lax.axis_index("sx"), lax.axis_index("sy"), lax.axis_index("cr")
    me_low, me_high = lax.rem(me_x, low), me_x // low
    nx = ids_ref.shape[0]
    nc = out_a.shape[1]
    steps = ncr // 2
    load_adj = pltpu.make_async_copy(adj_hbm, wide, local_sem.at[0])
    load_rows = pltpu.make_async_copy(rows_hbm, raw, local_sem.at[1])
    load_adj.start()
    load_rows.start()

    sides = []
    for dx in (-1, 0, 1):
        for dy in (-1, 0, 1):
            if dx or dy:
                x, y = me_x + dx, me_y + dy
                sides.append((dx, dy, (x >= 0) & (x < nsx) & (y >= 0) & (y < nsy), (x, y, me_z)))
    up = (me_x, me_y, lax.rem(me_z + 1, ncr))
    down = (me_x, me_y, lax.rem(me_z + ncr - 1, ncr))

    barrier = pltpu.get_barrier_semaphore()

    def greet(*device):
        pl.semaphore_signal(barrier, inc=1, device_id=device, device_id_type=MESH)

    greet(*up)
    greet(*down)
    for q in range(low):
        pl.when(q != me_low)(functools.partial(greet, me_high * low + q, me_y, me_z))
    for h in range(2):
        for y in range(nsy):
            pl.when((h != me_high) | (y != me_y))(functools.partial(greet, h * low + me_low, y, me_z))
    for dx in (-1, 1):
        for dy in (-1, 1):
            greet(lax.rem(me_x + nsx + dx, nsx), lax.rem(me_y + nsy + dy, nsy), me_z)
    first_low, last_low = me_low == 0, me_low == low - 1
    pl.when(first_low)(functools.partial(greet, lax.rem(me_x + nsx - 1, nsx), me_y, me_z))
    pl.when(last_low)(functools.partial(greet, lax.rem(me_x + 1, nsx), me_y, me_z))
    peers = 2 + (low - 1) + (2 * nsy - 1) + 4

    own_cond(ids_ref, mat_cond, scaled, unscaled)
    ids[1, DEG : DEG + nx] = ids_ref[...]
    load_adj.wait()
    load_own(wide, scaled, main, acc, coef)
    pack_edges(main, packed, nx)

    @pl.when(first_low | last_low)
    def _():
        pl.semaphore_wait(barrier, peers + 1)

    @pl.when(jnp.logical_not(first_low | last_low))
    def _():
        pl.semaphore_wait(barrier, peers)

    def rows_from(d):
        return {-1: (0, 8), 0: (0, nx), 1: (nx - 8, nx)}[d]

    def rows_to(d):
        return {-1: (DEG + nx, 2 * DEG + nx), 0: (DEG, DEG + nx), 1: (0, 8)}[d]

    halos = []
    for i, (dx, dy, there, device) in enumerate(sides):
        (a, b), (c, d) = rows_from(dx), rows_to(dx)
        if dy == 0:
            src = main.at[0, DEG + a : DEG + b]
            dst = main.at[0, c:d]
        else:
            src = packed.at[0 if dy < 0 else 1, a // 8 : b // 8]
            dst = got.at[1 if dy < 0 else 0, c // 8 : d // 8]
        halos.append((there, [
            pltpu.make_async_remote_copy(
                src_ref=src, dst_ref=dst, send_sem=halo_send.at[0, i], recv_sem=halo_recv.at[0, i],
                device_id=device, device_id_type=MESH),
            pltpu.make_async_remote_copy(
                src_ref=ids_ref.at[a:b], dst_ref=ids.at[1 - dy, c:d], send_sem=halo_send.at[1, i],
                recv_sem=halo_recv.at[1, i], device_id=device, device_id_type=MESH),
        ]))

    order = sorted(range(8), key=lambda i: abs(sides[i][1]))
    for i in order:
        there, copies = halos[i]

        @pl.when(there)
        def _(copies=copies):
            copies[0].start()
            copies[1].start()

    for i, (dx, dy, there, device) in enumerate(sides):
        c, d = rows_to(-dx)

        @pl.when(jnp.logical_not(there))
        def _(dx=dx, dy=dy, c=c, d=d):
            ids[1 + dy, c:d] = jnp.full((d - c, LANES), -1, jnp.int32)
            if dy == 0:
                main[0, c:d] = jnp.zeros((d - c, 2, 8, LANES), jnp.float32)
            else:
                got[0 if dy < 0 else 1, c // 8 : d // 8] = jnp.zeros(((d - c) // 8, 8, LANES), jnp.float32)

    load_rows.wait()
    turn_rows(raw, flat)

    for i, (dx, dy, there, device) in enumerate(sides):
        there_copies = halos[7 - i][1]

        @pl.when(there)
        def _(mine=halos[i][1], theirs=there_copies):
            for copy in mine:
                copy.wait_send()
            for copy in theirs:
                copy.wait_recv()

    build_fields(ids, mat_diag, mat_cond, diag2, cond2)
    unpack_edges(got, side)
    filter_steps(main, side, diag2, cond2, acc, coef, nx)
    finish(acc, unscaled, smooth, cols, nx)

    def hop(way, s, p):
        last = s == steps
        here = 0 if s == 1 else 2 * (s - 1) - 1 + way
        slot = 2 * s - 1 if last else 2 * s - 1 + way
        return pltpu.make_async_remote_copy(
            src_ref=cols.at[p, here], dst_ref=cols.at[p, slot], send_sem=z_send.at[way, s - 1, p],
            recv_sem=z_recv.at[way, s - 1, p], device_id=up if way == 0 else down, device_id_type=MESH)

    def hops(s):
        return [(way, p) for p in range(PIECES) for way in range(2)
                if s < steps or p % 2 == way]

    for way, p in hops(1):
        hop(way, 1, p).start()
    store = pltpu.make_async_copy(smooth, smooth_hbm, local_sem.at[2])
    store.start()

    def arrive(s):
        for way, p in hops(s):
            hop(way, s, p).wait_recv()
            if s < steps and (way, p) in hops(s + 1):
                hop(way, s + 1, p).start()

    def block_of(slot):
        s = (slot + 1) // 2
        return lax.rem(me_z + ncr - s, ncr) if slot % 2 else lax.rem(me_z + s, ncr)

    def multiply(first, last, half):
        count = (last - first) * nc
        wide_rows = flat.shape[0] // 2
        depth = cols.shape[-1]
        total = None
        for p in range(PIECES):
            lhs = cols[p, first:last].reshape(count, depth)
            rhs = flat[half * wide_rows : (half + 1) * wide_rows, p * depth : (p + 1) * depth]
            part = lax.dot_general(lhs, rhs, (((1,), (1,)), ((), ())), preferred_element_type=jnp.float32)
            total = part if total is None else total + part
        out_a[first:last, :, half * wide_rows : (half + 1) * wide_rows] = total.astype(jnp.bfloat16).reshape(
            last - first, nc, wide_rows)

    def send_a(slot):
        block = block_of(slot)
        to_low, high = lax.rem(block, low), block // low
        return to_low, high, pltpu.make_async_remote_copy(
            src_ref=out_a.at[slot], dst_ref=in_a.at[high, me_low], send_sem=a_send.at[slot],
            recv_sem=a_recv.at[high, me_low], device_id=(me_high * low + to_low, me_y, me_z), device_id_type=MESH)

    def share(first, last):
        for slot in range(first, last):
            to_low, high, copy = send_a(slot)
            pl.when(to_low != me_low)(copy.start)

            @pl.when(to_low == me_low)
            def _(slot=slot, high=high):
                in_a[high, me_low] = out_a[slot]

    def send_b(h, y):
        return pltpu.make_async_remote_copy(
            src_ref=out_b.at[h, y], dst_ref=in_b.at[me_high * nsy + me_y], send_sem=b_send.at[h, y],
            recv_sem=b_recv.at[me_high * nsy + me_y], device_id=(h * low + me_low, y, me_z), device_id_type=MESH)

    def gather_a(h):
        for q in range(low):
            @pl.when(q != me_low)
            def _(q=q):
                pltpu.make_async_remote_copy(
                    src_ref=out_a.at[0], dst_ref=in_a.at[h, q], send_sem=a_send.at[0],
                    recv_sem=a_recv.at[h, q], device_id=(me_high * low + q, me_y, me_z),
                    device_id_type=MESH).wait_recv()
        total = in_a[h, 0].astype(jnp.float32)
        for q in range(1, low):
            total = total + in_a[h, q].astype(jnp.float32)
        oc = nc // nsy
        for y in range(nsy):
            out_b[h, y] = total[y * oc : (y + 1) * oc]
        for y in range(nsy):
            mine = (h == me_high) & (y == me_y)
            pl.when(jnp.logical_not(mine))(send_b(h, y).start)

            @pl.when(mine)
            def _(y=y):
                in_b[me_high * nsy + me_y] = out_b[h, y]

    early = lax.rem(me_low - me_z + ncr + ncr // 4, ncr) // (ncr // 2 + 1)

    groups = []
    s = steps
    while s > 0:
        before = max(s - 2, 0)
        groups.append((before, s))
        s = before
    groups.reverse()
    for n, (before, last_step) in enumerate(groups):
        first = 0 if before == 0 else 2 * before + 1
        last = 2 * last_step + 1 if last_step < steps else 2 * steps
        arrive(before + 1)
        if n:
            multiply(pending[0], pending[1], 0)
        if before + 2 <= last_step:
            arrive(before + 2)
        if n:
            multiply(pending[0], pending[1], 1)
            share(pending[0], pending[1])
        pending = (first, last)
    gather_a(early)
    multiply(pending[0], pending[1], 0)
    multiply(pending[0], pending[1], 1)
    share(pending[0], pending[1])
    gather_a(1 - early)
    for peer in range(2 * nsy):
        h, y = peer // nsy, peer % nsy

        @pl.when((h != me_high) | (y != me_y))
        def _(peer=peer, h=h, y=y):
            pltpu.make_async_remote_copy(
                src_ref=out_b.at[0, 0], dst_ref=in_b.at[peer], send_sem=b_send.at[0, 0],
                recv_sem=b_recv.at[peer], device_id=(h * low + me_low, y, me_z), device_id_type=MESH).wait_recv()
    total = in_b[0]
    for peer in range(1, 2 * nsy):
        total = total + in_b[peer]
    panel_ref[...] = total

    for s in range(1, steps + 1):
        for way, p in hops(s):
            hop(way, s, p).wait_send()
    for slot in range(2 * steps):
        to_low, high, copy = send_a(slot)
        pl.when(to_low != me_low)(copy.wait_send)
    for h in range(2):
        for y in range(nsy):
            pl.when((h != me_high) | (y != me_y))(send_b(h, y).wait_send)
    store.wait()


def on_device(sizes, adjoint, sensor_rows, cell_ids, mat_diag, mat_cond, cheb_coef):
    nsx, nsy, ncr = sizes
    nc, nx, ny = adjoint.shape
    nr = sensor_rows.shape[0]
    low = nsx // 2
    wide = nx + 2 * DEG
    oc = nc // nsy
    f32, bf16 = jnp.float32, jnp.bfloat16
    vmem = pl.BlockSpec(memory_space=pltpu.VMEM)
    smem = pl.BlockSpec(memory_space=pltpu.SMEM)
    hbm = pl.BlockSpec(memory_space=pl.ANY)
    dma = pltpu.SemaphoreType.DMA
    smooth, panel = pl.pallas_call(
        functools.partial(kernel, sizes),
        out_shape=(jax.ShapeDtypeStruct((nc * nx, ny), f32), jax.ShapeDtypeStruct((oc, nr), f32)),
        in_specs=[hbm, hbm, vmem, smem, smem, smem],
        out_specs=(hbm, vmem),
        scratch_shapes=[
            pltpu.VMEM((nc * nx, ny), f32),
            pltpu.VMEM((nr, nx, ny), bf16),
            pltpu.VMEM((nr, nx * ny), bf16),
            pltpu.VMEM((3, wide, ny), jnp.int32),
            pltpu.VMEM((2, nx, 8, ny), f32),
            pltpu.VMEM((2, nx, 8, ny), f32),
            pltpu.VMEM((2, wide, 2, 8, ny), f32),
            pltpu.VMEM((2, wide, 8, ny), f32),
            pltpu.VMEM((nx, 2, 8, ny), f32),
            pltpu.VMEM((2, nx // 8, 8, ny), f32),
            pltpu.VMEM((2, wide // 8, 8, ny), f32),
            pltpu.VMEM((3, wide, 8, ny), f32),
            pltpu.VMEM((3, wide, 8, ny), f32),
            pltpu.VMEM((nc * nx, ny), f32),
            pltpu.VMEM((PIECES, ncr, nc, nx * ny // PIECES), bf16),
            pltpu.VMEM((ncr, nc, nr), bf16),
            pltpu.VMEM((2, low, nc, nr), bf16),
            pltpu.VMEM((2, nsy, oc, nr), f32),
            pltpu.VMEM((2 * nsy, oc, nr), f32),
            dma((3,)),
            dma((2, 8)),
            dma((2, 8)),
            dma((2, ncr // 2, PIECES)),
            dma((2, ncr // 2, PIECES)),
            dma((ncr,)),
            dma((2, low)),
            dma((2, nsy)),
            dma((2 * nsy,)),
        ],
        compiler_params=pltpu.CompilerParams(
            collective_id=0, has_side_effects=True, vmem_limit_bytes=62 << 20
        ),
    )(adjoint.reshape(nc * nx, ny), sensor_rows, cell_ids, mat_diag, mat_cond, cheb_coef)
    return smooth.reshape(nc, nx, ny), panel.T


def solution(mesh):
    placed = (P("cr", "sx", "sy"), P("cr", "sx", "sy"), P("sx", "sy"), P(), P(), P())
    sizes = tuple(mesh.shape[axis] for axis in ("sx", "sy", "cr"))
    return jax.shard_map(
        functools.partial(on_device, sizes),
        mesh=mesh,
        in_specs=placed,
        out_specs=(P("cr", "sx", "sy"), P("cr", ("sx", "sy"))),
        check_vma=False,
    )
```

```python
import functools

import jax
import jax.numpy as jnp
from jax import lax
from jax.experimental import pallas as pl
from jax.experimental.pallas import tpu as pltpu
from jax.sharding import PartitionSpec as P

DEG = 8
LANES = 128
HALF = LANES // 2
PIECES = 2
MESH = pl.DeviceIdType.MESH


def lane_iota(shape):
    return lax.broadcasted_iota(jnp.int32, shape, len(shape) - 1)


def roll(value, shift):
    return pltpu.roll(value, shift % LANES, value.ndim - 1)


def lookup(ids, table):
    out = jnp.zeros(ids.shape, jnp.float32)
    for material in range(table.shape[0]):
        out = jnp.where(ids == material, table[material], out)
    return out


def load_own(wide, scaled, main, acc, coef):
    nx = scaled.shape[1]
    for x in range(nx):
        for g in range(2):
            value = wide[pl.ds(g * 8 * nx + x, 8, stride=nx), :]
            if g == 1:
                value = roll(value, HALF)
            value = scaled[g, x] * value
            main[0, DEG + x, g] = value
            acc[x, g] = coef[0] * value


def pack_edges(main, packed, nx):
    lane = lane_iota((8, LANES))
    window = lax.rem(lane, HALF) // DEG
    low = lane < HALF
    for xb in range(nx // 8):
        first = jnp.zeros((8, LANES), jnp.float32)
        last = jnp.zeros((8, LANES), jnp.float32)
        for i in range(8):
            m0 = main[0, DEG + 8 * xb + i, 0]
            m1 = main[0, DEG + 8 * xb + i, 1]
            first = jnp.where(window == i, roll(jnp.where(low, m0, m1), 8 * i), first)
            last = jnp.where(window == i, roll(jnp.where(low, m1, m0), 8 * (i + 1)), last)
        packed[0, xb] = first
        packed[1, xb] = last


def thin_edges(main, thin, nx):
    for e, start in enumerate((DEG, nx)):
        for x in range(8):
            thin[e, x] = main[0, start + x].reshape(16, LANES).astype(jnp.bfloat16)


def widen_edges(thin_got, main, nx):
    for e, start in enumerate((0, DEG + nx)):
        for x in range(8):
            main[0, start + x] = thin_got[e, x].astype(jnp.float32).reshape(2, 8, LANES)


def unpack_edges(got, side):
    lane = lax.rem(lane_iota((8, LANES)), HALF)
    for xb in range(got.shape[1]):
        left = got[0, xb]
        right = got[1, xb]
        for i in range(8):
            value = jnp.where(lane >= HALF - DEG, roll(left, -8 * (i + 1)), 0.0)
            side[0, 8 * xb + i] = jnp.where(lane < DEG, roll(right, -8 * i), value)


def build_fields(ids, mat_diag, mat_cond, diag2, cond2):
    middle = ids[1]
    rows = middle.shape[0]
    lane = lane_iota((rows, LANES))
    in_half = lax.rem(lane, HALF)
    lower = lane < HALF
    left = jnp.where(lower, roll(ids[0], HALF), ids[0])
    right = jnp.where(lower, ids[2], roll(ids[2], HALF))
    edges = jnp.where(in_half < DEG, right, jnp.where(in_half >= HALF - DEG, left, -1))
    for t, tile in enumerate((middle, None, edges)):
        if tile is None:
            d, c = roll(diag, HALF), roll(cond, HALF)
        else:
            diag, cond = lookup(tile, mat_diag), lookup(tile, mat_cond)
            d, c = diag, cond
        diag2[t] = jnp.broadcast_to((2.0 * d)[:, None, :], (rows, 8, LANES))
        cond2[t] = jnp.broadcast_to((2.0 * c * c)[:, None, :], (rows, 8, LANES))


def own_cond(ids_ref, mat_cond, scaled, unscaled):
    cond = lookup(ids_ref[...], mat_cond)
    nx = cond.shape[0]
    for g in range(2):
        value = cond if g == 0 else roll(cond, HALF)
        scaled[g] = jnp.broadcast_to(value[:, None, :], (nx, 8, LANES))
        unscaled[g] = jnp.broadcast_to((1.0 / value)[:, None, :], (nx, 8, LANES))


def filter_steps(main, side, diag2, cond2, acc, coef, nx):
    rows = nx + 2 * DEG
    for k in range(1, DEG + 1):
        cur, new = (k + 1) % 2, k % 2
        cuts = [k] + [c for c in range(8, rows, 8) if k < c < rows - k] + [rows - k]
        for a, b in zip(cuts[:-1], cuts[1:]):
            lane = lane_iota((b - a, 8, LANES))
            whole = [main[cur, a - 1 : b + 1, 0], main[cur, a - 1 : b + 1, 1], side[cur, a - 1 : b + 1]]
            middle = [w[1:-1] for w in whole]
            before = [roll(m, 1) for m in middle]
            after = [roll(m, -1) for m in middle]
            wrap_b = (0, HALF)
            wrap_a = (LANES - 1, HALF - 1)
            for t in range(3 if k < DEG else 2):
                if t < 2:
                    lhs = jnp.where(lane == wrap_b[t], before[2], before[t])
                    rhs = jnp.where(lane == wrap_a[t], after[2], after[t])
                else:
                    lhs = jnp.where(lane == wrap_b[0], before[0], jnp.where(lane == wrap_b[1], before[1], before[2]))
                    rhs = jnp.where(lane == wrap_a[0], after[0], jnp.where(lane == wrap_a[1], after[1], after[2]))
                beside = (whole[t][:-2] + whole[t][2:]) + (lhs + rhs)
                value = diag2[t, a:b] * middle[t] + cond2[t, a:b] * beside
                if k == 1:
                    value = 0.5 * value
                elif t < 2:
                    value = value - main[new, a:b, t]
                else:
                    value = value - side[new, a:b]
                if t == 2:
                    side[new, a:b] = value
                else:
                    if k < DEG:
                        main[new, a:b, t] = value
                    if a >= DEG and b <= rows - DEG:
                        acc[a - DEG : b - DEG, t] = acc[a - DEG : b - DEG, t] + coef[k] * value


def finish(acc, unscaled, smooth, cols, nx):
    depth = cols.shape[-1]
    for x in range(nx):
        done = []
        for g in range(2):
            value = acc[x, g] * unscaled[g, x]
            if g == 1:
                value = roll(value, HALF)
            smooth[pl.ds(g * 8 * nx + x, 8, stride=nx), :] = value
            done.append(value)
        at = x * LANES
        cols[at // depth, 0, :, at % depth : at % depth + LANES] = jnp.concatenate(done, axis=0).astype(jnp.bfloat16)


def turn_rows(raw, flat):
    step = 16
    nx = raw.shape[1]

    def body(i, carry):
        at = pl.ds(pl.multiple_of(i * step, step), step)
        turned = jnp.swapaxes(raw[at], 0, 1)
        for x in range(nx):
            flat[at, x * LANES : (x + 1) * LANES] = turned[x]
        return carry

    lax.fori_loop(0, raw.shape[0] // step, body, 0)


def kernel(
    sizes,
    adj_hbm, rows_hbm, ids_ref, mat_diag, mat_cond, coef,
    smooth, panel_ref,
    wide, raw, flat, ids, scaled, unscaled, main, side, acc, packed, got, thin, thin_got, diag2, cond2, cols,
    out_a, in_a, out_b, in_b,
    local_sem, halo_send, halo_recv, z_send, z_recv, a_send, a_recv, b_send, b_recv,
):
    nsx, nsy, ncr = sizes
    low = nsx // 2
    me_x, me_y, me_z = lax.axis_index("sx"), lax.axis_index("sy"), lax.axis_index("cr")
    me_low, me_high = lax.rem(me_x, low), me_x // low
    nx = ids_ref.shape[0]
    nc = out_a.shape[1]
    steps = ncr // 2
    load_adj = pltpu.make_async_copy(adj_hbm, wide, local_sem.at[0])
    load_rows = pltpu.make_async_copy(rows_hbm, raw, local_sem.at[1])
    load_adj.start()
    load_rows.start()

    sides = []
    for dx in (-1, 0, 1):
        for dy in (-1, 0, 1):
            if dx or dy:
                x, y = me_x + dx, me_y + dy
                sides.append((dx, dy, (x >= 0) & (x < nsx) & (y >= 0) & (y < nsy), (x, y, me_z)))
    up = (me_x, me_y, lax.rem(me_z + 1, ncr))
    down = (me_x, me_y, lax.rem(me_z + ncr - 1, ncr))

    barrier = pltpu.get_barrier_semaphore()

    def greet(*device):
        pl.semaphore_signal(barrier, inc=1, device_id=device, device_id_type=MESH)

    greet(*up)
    greet(*down)
    for q in range(low):
        pl.when(q != me_low)(functools.partial(greet, me_high * low + q, me_y, me_z))
    for h in range(2):
        for y in range(nsy):
            pl.when((h != me_high) | (y != me_y))(functools.partial(greet, h * low + me_low, y, me_z))
    for dx in (-1, 1):
        for dy in (-1, 1):
            greet(lax.rem(me_x + nsx + dx, nsx), lax.rem(me_y + nsy + dy, nsy), me_z)
    first_low, last_low = me_low == 0, me_low == low - 1
    pl.when(first_low)(functools.partial(greet, lax.rem(me_x + nsx - 1, nsx), me_y, me_z))
    pl.when(last_low)(functools.partial(greet, lax.rem(me_x + 1, nsx), me_y, me_z))
    peers = 2 + (low - 1) + (2 * nsy - 1) + 4

    own_cond(ids_ref, mat_cond, scaled, unscaled)
    ids[1, DEG : DEG + nx] = ids_ref[...]
    load_adj.wait()
    load_own(wide, scaled, main, acc, coef)
    pack_edges(main, packed, nx)
    thin_edges(main, thin, nx)

    @pl.when(first_low | last_low)
    def _():
        pl.semaphore_wait(barrier, peers + 1)

    @pl.when(jnp.logical_not(first_low | last_low))
    def _():
        pl.semaphore_wait(barrier, peers)

    def rows_from(d):
        return {-1: (0, 8), 0: (0, nx), 1: (nx - 8, nx)}[d]

    def rows_to(d):
        return {-1: (DEG + nx, 2 * DEG + nx), 0: (DEG, DEG + nx), 1: (0, 8)}[d]

    halos = []
    for i, (dx, dy, there, device) in enumerate(sides):
        (a, b), (c, d) = rows_from(dx), rows_to(dx)
        if dy == 0:
            src = thin.at[0 if dx < 0 else 1]
            dst = thin_got.at[1 if dx < 0 else 0]
        else:
            src = packed.at[0 if dy < 0 else 1, a // 8 : b // 8]
            dst = got.at[1 if dy < 0 else 0, c // 8 : d // 8]
        halos.append((there, [
            pltpu.make_async_remote_copy(
                src_ref=src, dst_ref=dst, send_sem=halo_send.at[0, i], recv_sem=halo_recv.at[0, i],
                device_id=device, device_id_type=MESH),
            pltpu.make_async_remote_copy(
                src_ref=ids_ref.at[a:b], dst_ref=ids.at[1 - dy, c:d], send_sem=halo_send.at[1, i],
                recv_sem=halo_recv.at[1, i], device_id=device, device_id_type=MESH),
        ]))

    order = sorted(range(8), key=lambda i: abs(sides[i][1]))
    for i in order:
        there, copies = halos[i]

        @pl.when(there)
        def _(copies=copies):
            copies[0].start()
            copies[1].start()

    for i, (dx, dy, there, device) in enumerate(sides):
        c, d = rows_to(-dx)

        @pl.when(jnp.logical_not(there))
        def _(dx=dx, dy=dy, c=c, d=d):
            ids[1 + dy, c:d] = jnp.full((d - c, LANES), -1, jnp.int32)
            if dy == 0:
                thin_got[0 if dx < 0 else 1] = jnp.zeros((8, 16, LANES), jnp.bfloat16)
            else:
                got[0 if dy < 0 else 1, c // 8 : d // 8] = jnp.zeros(((d - c) // 8, 8, LANES), jnp.float32)

    for i, (dx, dy, there, device) in enumerate(sides):
        there_copies = halos[7 - i][1]

        @pl.when(there)
        def _(mine=halos[i][1], theirs=there_copies):
            for copy in mine:
                copy.wait_send()
            for copy in theirs:
                copy.wait_recv()

    build_fields(ids, mat_diag, mat_cond, diag2, cond2)
    unpack_edges(got, side)
    widen_edges(thin_got, main, nx)
    filter_steps(main, side, diag2, cond2, acc, coef, nx)
    finish(acc, unscaled, smooth, cols, nx)

    def hop(way, s, p):
        last = s == steps
        here = 0 if s == 1 else 2 * (s - 1) - 1 + way
        slot = 2 * s - 1 if last else 2 * s - 1 + way
        return pltpu.make_async_remote_copy(
            src_ref=cols.at[p, here], dst_ref=cols.at[p, slot], send_sem=z_send.at[way, s - 1, p],
            recv_sem=z_recv.at[way, s - 1, p], device_id=up if way == 0 else down, device_id_type=MESH)

    def hops(s):
        return [(way, p) for p in range(PIECES) for way in range(2)
                if s < steps or p % 2 == way]

    for way, p in hops(1):
        hop(way, 1, p).start()
    load_rows.wait()
    turn_rows(raw, flat)

    def arrive(s):
        for way, p in hops(s):
            hop(way, s, p).wait_recv()
            if s < steps and (way, p) in hops(s + 1):
                hop(way, s + 1, p).start()

    def block_of(slot):
        s = (slot + 1) // 2
        return lax.rem(me_z + ncr - s, ncr) if slot % 2 else lax.rem(me_z + s, ncr)

    def multiply(first, last):
        count = (last - first) * nc
        depth = cols.shape[-1]
        total = None
        for p in range(PIECES):
            lhs = cols[p, first:last].reshape(count, depth)
            rhs = flat[:, p * depth : (p + 1) * depth]
            part = lax.dot_general(lhs, rhs, (((1,), (1,)), ((), ())), preferred_element_type=jnp.float32)
            total = part if total is None else total + part
        out_a[first:last] = total.astype(jnp.bfloat16).reshape(last - first, nc, flat.shape[0])

    def send_a(slot):
        block = block_of(slot)
        to_low, high = lax.rem(block, low), block // low
        return to_low, high, pltpu.make_async_remote_copy(
            src_ref=out_a.at[slot], dst_ref=in_a.at[high, me_low], send_sem=a_send.at[slot],
            recv_sem=a_recv.at[high, me_low], device_id=(me_high * low + to_low, me_y, me_z), device_id_type=MESH)

    def share(first, last):
        for slot in range(first, last):
            to_low, high, copy = send_a(slot)
            pl.when(to_low != me_low)(copy.start)

            @pl.when(to_low == me_low)
            def _(slot=slot, high=high):
                in_a[high, me_low] = out_a[slot]

    def send_b(h, y):
        return pltpu.make_async_remote_copy(
            src_ref=out_b.at[h, y], dst_ref=in_b.at[me_high * nsy + me_y], send_sem=b_send.at[h, y],
            recv_sem=b_recv.at[me_high * nsy + me_y], device_id=(h * low + me_low, y, me_z), device_id_type=MESH)

    def gather_a(h):
        for q in range(low):
            @pl.when(q != me_low)
            def _(q=q):
                pltpu.make_async_remote_copy(
                    src_ref=out_a.at[0], dst_ref=in_a.at[h, q], send_sem=a_send.at[0],
                    recv_sem=a_recv.at[h, q], device_id=(me_high * low + q, me_y, me_z),
                    device_id_type=MESH).wait_recv()
        total = in_a[h, 0].astype(jnp.float32)
        for q in range(1, low):
            total = total + in_a[h, q].astype(jnp.float32)
        oc = nc // nsy
        for y in range(nsy):
            out_b[h, y] = total[y * oc : (y + 1) * oc]
        for y in range(nsy):
            mine = (h == me_high) & (y == me_y)
            pl.when(jnp.logical_not(mine))(send_b(h, y).start)

            @pl.when(mine)
            def _(y=y):
                in_b[me_high * nsy + me_y] = out_b[h, y]

    early = lax.rem(me_low - me_z + ncr + ncr // 4, ncr) // (ncr // 2 + 1)

    for s in range(1, steps + 1):
        first = 0 if s == 1 else 2 * s - 1
        last = min(2 * s + 1, 2 * steps)
        arrive(s)
        multiply(first, last)
        share(first, last)
        if s == steps - 1:
            gather_a(early)
    gather_a(1 - early)
    for peer in range(2 * nsy):
        h, y = peer // nsy, peer % nsy

        @pl.when((h != me_high) | (y != me_y))
        def _(peer=peer, h=h, y=y):
            pltpu.make_async_remote_copy(
                src_ref=out_b.at[0, 0], dst_ref=in_b.at[peer], send_sem=b_send.at[0, 0],
                recv_sem=b_recv.at[peer], device_id=(h * low + me_low, y, me_z), device_id_type=MESH).wait_recv()
    total = in_b[0]
    for peer in range(1, 2 * nsy):
        total = total + in_b[peer]
    panel_ref[...] = total

    for s in range(1, steps + 1):
        for way, p in hops(s):
            hop(way, s, p).wait_send()
    for slot in range(2 * steps):
        to_low, high, copy = send_a(slot)
        pl.when(to_low != me_low)(copy.wait_send)
    for h in range(2):
        for y in range(nsy):
            pl.when((h != me_high) | (y != me_y))(send_b(h, y).wait_send)


def write_out(smooth, panel, smooth_out, panel_out, sem):
    copies = [
        pltpu.make_async_copy(smooth, smooth_out, sem.at[0]),
        pltpu.make_async_copy(panel, panel_out, sem.at[1]),
    ]
    for copy in copies:
        copy.start()
    for copy in copies:
        copy.wait()


def on_device(sizes, adjoint, sensor_rows, cell_ids, mat_diag, mat_cond, cheb_coef):
    nsx, nsy, ncr = sizes
    nc, nx, ny = adjoint.shape
    nr = sensor_rows.shape[0]
    low = nsx // 2
    wide = nx + 2 * DEG
    oc = nc // nsy
    f32, bf16 = jnp.float32, jnp.bfloat16
    vmem = pl.BlockSpec(memory_space=pltpu.VMEM)
    smem = pl.BlockSpec(memory_space=pltpu.SMEM)
    hbm = pl.BlockSpec(memory_space=pl.ANY)
    dma = pltpu.SemaphoreType.DMA
    smooth, panel = pl.pallas_call(
        functools.partial(kernel, sizes),
        out_shape=(jax.ShapeDtypeStruct((nc * nx, ny), f32), jax.ShapeDtypeStruct((oc, nr), f32)),
        in_specs=[hbm, hbm, vmem, smem, smem, smem],
        out_specs=(vmem, vmem),
        scratch_shapes=[
            pltpu.VMEM((nc * nx, ny), f32),
            pltpu.VMEM((nr, nx, ny), bf16),
            pltpu.VMEM((nr, nx * ny), bf16),
            pltpu.VMEM((3, wide, ny), jnp.int32),
            pltpu.VMEM((2, nx, 8, ny), f32),
            pltpu.VMEM((2, nx, 8, ny), f32),
            pltpu.VMEM((2, wide, 2, 8, ny), f32),
            pltpu.VMEM((2, wide, 8, ny), f32),
            pltpu.VMEM((nx, 2, 8, ny), f32),
            pltpu.VMEM((2, nx // 8, 8, ny), f32),
            pltpu.VMEM((2, wide // 8, 8, ny), f32),
            pltpu.VMEM((2, 8, 16, ny), bf16),
            pltpu.VMEM((2, 8, 16, ny), bf16),
            pltpu.VMEM((3, wide, 8, ny), f32),
            pltpu.VMEM((3, wide, 8, ny), f32),
            pltpu.VMEM((PIECES, ncr, nc, nx * ny // PIECES), bf16),
            pltpu.VMEM((ncr, nc, nr), bf16),
            pltpu.VMEM((2, low, nc, nr), bf16),
            pltpu.VMEM((2, nsy, oc, nr), f32),
            pltpu.VMEM((2 * nsy, oc, nr), f32),
            dma((2,)),
            dma((2, 8)),
            dma((2, 8)),
            dma((2, ncr // 2, PIECES)),
            dma((2, ncr // 2, PIECES)),
            dma((ncr,)),
            dma((2, low)),
            dma((2, nsy)),
            dma((2 * nsy,)),
        ],
        compiler_params=pltpu.CompilerParams(
            collective_id=0, has_side_effects=True, vmem_limit_bytes=62 << 20
        ),
    )(adjoint.reshape(nc * nx, ny), sensor_rows, cell_ids, mat_diag, mat_cond, cheb_coef)
    smooth, panel = pl.pallas_call(
        write_out,
        out_shape=(jax.ShapeDtypeStruct(smooth.shape, f32), jax.ShapeDtypeStruct(panel.shape, f32)),
        in_specs=[vmem, vmem],
        out_specs=(hbm, hbm),
        scratch_shapes=[dma((2,))],
    )(smooth, panel)
    return smooth.reshape(nc, nx, ny), panel.T


def solution(mesh):
    placed = (P("cr", "sx", "sy"), P("cr", "sx", "sy"), P("sx", "sy"), P(), P(), P())
    sizes = tuple(mesh.shape[axis] for axis in ("sx", "sy", "cr"))
    return jax.shard_map(
        functools.partial(on_device, sizes),
        mesh=mesh,
        in_specs=placed,
        out_specs=(P("cr", "sx", "sy"), P("cr", ("sx", "sy"))),
        check_vma=False,
    )
```

```python
import functools

import jax
import jax.numpy as jnp
from jax import lax
from jax.experimental import pallas as pl
from jax.experimental.pallas import tpu as pltpu
from jax.sharding import PartitionSpec as P

DEG = 8
LANES = 128
HALF = LANES // 2
PIECES = 2
MESH = pl.DeviceIdType.MESH


def lane_iota(shape):
    return lax.broadcasted_iota(jnp.int32, shape, len(shape) - 1)


def roll(value, shift):
    return pltpu.roll(value, shift % LANES, value.ndim - 1)


def lookup(ids, table):
    out = jnp.zeros(ids.shape, jnp.float32)
    for material in range(table.shape[0]):
        out = jnp.where(ids == material, table[material], out)
    return out


def load_own(wide, scaled, main, acc, coef):
    nx = scaled.shape[1]
    for x in range(nx):
        for g in range(2):
            value = wide[pl.ds(g * 8 * nx + x, 8, stride=nx), :]
            if g == 1:
                value = roll(value, HALF)
            value = scaled[g, x] * value
            main[0, DEG + x, g] = value
            acc[x, g] = coef[0] * value


def pack_edges(main, packed, nx):
    lane = lane_iota((8, LANES))
    window = lax.rem(lane, HALF) // DEG
    low = lane < HALF
    for xb in range(nx // 8):
        first = jnp.zeros((8, LANES), jnp.float32)
        last = jnp.zeros((8, LANES), jnp.float32)
        for i in range(8):
            m0 = main[0, DEG + 8 * xb + i, 0]
            m1 = main[0, DEG + 8 * xb + i, 1]
            first = jnp.where(window == i, roll(jnp.where(low, m0, m1), 8 * i), first)
            last = jnp.where(window == i, roll(jnp.where(low, m1, m0), 8 * (i + 1)), last)
        packed[0, xb] = first
        packed[1, xb] = last


def thin_edges(main, thin, nx):
    for e, start in enumerate((DEG, nx)):
        for x in range(8):
            thin[e, x] = main[0, start + x].reshape(16, LANES).astype(jnp.bfloat16)


def widen_edges(thin_got, main, nx):
    for e, start in enumerate((0, DEG + nx)):
        for x in range(8):
            main[0, start + x] = thin_got[e, x].astype(jnp.float32).reshape(2, 8, LANES)


def unpack_edges(got, side):
    lane = lax.rem(lane_iota((8, LANES)), HALF)
    for xb in range(got.shape[1]):
        left = got[0, xb]
        right = got[1, xb]
        for i in range(8):
            value = jnp.where(lane >= HALF - DEG, roll(left, -8 * (i + 1)), 0.0)
            side[0, 8 * xb + i] = jnp.where(lane < DEG, roll(right, -8 * i), value)


def build_fields(ids, mat_diag, mat_cond, diag2, cond2):
    middle = ids[1]
    rows = middle.shape[0]
    lane = lane_iota((rows, LANES))
    in_half = lax.rem(lane, HALF)
    lower = lane < HALF
    left = jnp.where(lower, roll(ids[0], HALF), ids[0])
    right = jnp.where(lower, ids[2], roll(ids[2], HALF))
    edges = jnp.where(in_half < DEG, right, jnp.where(in_half >= HALF - DEG, left, -1))
    for t, tile in enumerate((middle, None, edges)):
        if tile is None:
            d, c = roll(diag, HALF), roll(cond, HALF)
        else:
            diag, cond = lookup(tile, mat_diag), lookup(tile, mat_cond)
            d, c = diag, cond
        diag2[t] = jnp.broadcast_to((2.0 * d)[:, None, :], (rows, 8, LANES))
        cond2[t] = jnp.broadcast_to((2.0 * c * c)[:, None, :], (rows, 8, LANES))


def own_cond(ids_ref, mat_cond, scaled, unscaled):
    cond = lookup(ids_ref[...], mat_cond)
    nx = cond.shape[0]
    for g in range(2):
        value = cond if g == 0 else roll(cond, HALF)
        scaled[g] = jnp.broadcast_to(value[:, None, :], (nx, 8, LANES))
        unscaled[g] = jnp.broadcast_to((1.0 / value)[:, None, :], (nx, 8, LANES))


def filter_steps(main, side, diag2, cond2, acc, coef, nx):
    rows = nx + 2 * DEG
    for k in range(1, DEG + 1):
        cur, new = (k + 1) % 2, k % 2
        cuts = [k] + [c for c in range(8, rows, 8) if k < c < rows - k] + [rows - k]
        for a, b in zip(cuts[:-1], cuts[1:]):
            lane = lane_iota((b - a, 8, LANES))
            whole = [main[cur, a - 1 : b + 1, 0], main[cur, a - 1 : b + 1, 1], side[cur, a - 1 : b + 1]]
            middle = [w[1:-1] for w in whole]
            before = [roll(m, 1) for m in middle]
            after = [roll(m, -1) for m in middle]
            wrap_b = (0, HALF)
            wrap_a = (LANES - 1, HALF - 1)
            for t in range(3 if k < DEG else 2):
                if t < 2:
                    lhs = jnp.where(lane == wrap_b[t], before[2], before[t])
                    rhs = jnp.where(lane == wrap_a[t], after[2], after[t])
                else:
                    lhs = jnp.where(lane == wrap_b[0], before[0], jnp.where(lane == wrap_b[1], before[1], before[2]))
                    rhs = jnp.where(lane == wrap_a[0], after[0], jnp.where(lane == wrap_a[1], after[1], after[2]))
                beside = (whole[t][:-2] + whole[t][2:]) + (lhs + rhs)
                value = diag2[t, a:b] * middle[t] + cond2[t, a:b] * beside
                if k == 1:
                    value = 0.5 * value
                elif t < 2:
                    value = value - main[new, a:b, t]
                else:
                    value = value - side[new, a:b]
                if t == 2:
                    side[new, a:b] = value
                else:
                    if k < DEG:
                        main[new, a:b, t] = value
                    if a >= DEG and b <= rows - DEG:
                        acc[a - DEG : b - DEG, t] = acc[a - DEG : b - DEG, t] + coef[k] * value


def finish(part, acc, unscaled, smooth, cols, nx):
    depth = cols.shape[-1]
    count = depth // LANES
    for x in range(part * count, (part + 1) * count):
        done = []
        for g in range(2):
            value = acc[x, g] * unscaled[g, x]
            if g == 1:
                value = roll(value, HALF)
            smooth[pl.ds(g * 8 * nx + x, 8, stride=nx), :] = value
            done.append(value)
        at = x * LANES
        cols[at // depth, 0, :, at % depth : at % depth + LANES] = jnp.concatenate(done, axis=0).astype(jnp.bfloat16)


def turn_rows(raw, flat):
    step = 16
    nx = raw.shape[1]

    def body(i, carry):
        at = pl.ds(pl.multiple_of(i * step, step), step)
        turned = jnp.swapaxes(raw[at], 0, 1)
        for x in range(nx):
            flat[at, x * LANES : (x + 1) * LANES] = turned[x]
        return carry

    lax.fori_loop(0, raw.shape[0] // step, body, 0)


def kernel(
    sizes,
    adj_hbm, rows_hbm, ids_ref, mat_diag, mat_cond, coef,
    smooth, panel_ref,
    wide, raw, flat, ids, scaled, unscaled, main, side, acc, packed, got, thin, thin_got, diag2, cond2, cols,
    out_a, in_a, out_b, in_b,
    local_sem, halo_send, halo_recv, z_send, z_recv, a_send, a_recv, b_send, b_recv,
):
    nsx, nsy, ncr = sizes
    low = nsx // 2
    me_x, me_y, me_z = lax.axis_index("sx"), lax.axis_index("sy"), lax.axis_index("cr")
    me_low, me_high = lax.rem(me_x, low), me_x // low
    nx = ids_ref.shape[0]
    nc = out_a.shape[1]
    steps = ncr // 2
    load_adj = pltpu.make_async_copy(adj_hbm, wide, local_sem.at[0])
    load_rows = pltpu.make_async_copy(rows_hbm, raw, local_sem.at[1])
    load_adj.start()
    load_rows.start()

    sides = []
    for dx in (-1, 0, 1):
        for dy in (-1, 0, 1):
            if dx or dy:
                x, y = me_x + dx, me_y + dy
                sides.append((dx, dy, (x >= 0) & (x < nsx) & (y >= 0) & (y < nsy), (x, y, me_z)))
    up = (me_x, me_y, lax.rem(me_z + 1, ncr))
    down = (me_x, me_y, lax.rem(me_z + ncr - 1, ncr))

    barrier = pltpu.get_barrier_semaphore()

    def greet(*device):
        pl.semaphore_signal(barrier, inc=1, device_id=device, device_id_type=MESH)

    for dx in (-1, 1):
        for dy in (-1, 1):
            greet(lax.rem(me_x + nsx + dx, nsx), lax.rem(me_y + nsy + dy, nsy), me_z)
    first_low, last_low = me_low == 0, me_low == low - 1
    pl.when(first_low)(functools.partial(greet, lax.rem(me_x + nsx - 1, nsx), me_y, me_z))
    pl.when(last_low)(functools.partial(greet, lax.rem(me_x + 1, nsx), me_y, me_z))
    greet(*up)
    greet(*down)
    for q in range(low):
        pl.when(q != me_low)(functools.partial(greet, me_high * low + q, me_y, me_z))
    for h in range(2):
        for y in range(nsy):
            pl.when((h != me_high) | (y != me_y))(functools.partial(greet, h * low + me_low, y, me_z))
    peers = 2 + (low - 1) + (2 * nsy - 1) + 4

    own_cond(ids_ref, mat_cond, scaled, unscaled)
    ids[1, DEG : DEG + nx] = ids_ref[...]
    load_adj.wait()
    load_own(wide, scaled, main, acc, coef)
    pack_edges(main, packed, nx)
    thin_edges(main, thin, nx)

    @pl.when(first_low | last_low)
    def _():
        pl.semaphore_wait(barrier, peers + 1)

    @pl.when(jnp.logical_not(first_low | last_low))
    def _():
        pl.semaphore_wait(barrier, peers)

    def rows_from(d):
        return {-1: (0, 8), 0: (0, nx), 1: (nx - 8, nx)}[d]

    def rows_to(d):
        return {-1: (DEG + nx, 2 * DEG + nx), 0: (DEG, DEG + nx), 1: (0, 8)}[d]

    halos = []
    for i, (dx, dy, there, device) in enumerate(sides):
        (a, b), (c, d) = rows_from(dx), rows_to(dx)
        if dy == 0:
            src = thin.at[0 if dx < 0 else 1]
            dst = thin_got.at[1 if dx < 0 else 0]
        else:
            src = packed.at[0 if dy < 0 else 1, a // 8 : b // 8]
            dst = got.at[1 if dy < 0 else 0, c // 8 : d // 8]
        halos.append((there, [
            pltpu.make_async_remote_copy(
                src_ref=src, dst_ref=dst, send_sem=halo_send.at[0, i], recv_sem=halo_recv.at[0, i],
                device_id=device, device_id_type=MESH),
            pltpu.make_async_remote_copy(
                src_ref=ids_ref.at[a:b], dst_ref=ids.at[1 - dy, c:d], send_sem=halo_send.at[1, i],
                recv_sem=halo_recv.at[1, i], device_id=device, device_id_type=MESH),
        ]))

    order = sorted(range(8), key=lambda i: abs(sides[i][1]))
    for i in order:
        there, copies = halos[i]

        @pl.when(there)
        def _(copies=copies):
            copies[0].start()
            copies[1].start()

    for i, (dx, dy, there, device) in enumerate(sides):
        c, d = rows_to(-dx)

        @pl.when(jnp.logical_not(there))
        def _(dx=dx, dy=dy, c=c, d=d):
            ids[1 + dy, c:d] = jnp.full((d - c, LANES), -1, jnp.int32)
            if dy == 0:
                thin_got[0 if dx < 0 else 1] = jnp.zeros((8, 16, LANES), jnp.bfloat16)
            else:
                got[0 if dy < 0 else 1, c // 8 : d // 8] = jnp.zeros(((d - c) // 8, 8, LANES), jnp.float32)

    for i, (dx, dy, there, device) in enumerate(sides):
        there_copies = halos[7 - i][1]

        @pl.when(there)
        def _(mine=halos[i][1], theirs=there_copies):
            for copy in mine:
                copy.wait_send()
            for copy in theirs:
                copy.wait_recv()

    build_fields(ids, mat_diag, mat_cond, diag2, cond2)
    unpack_edges(got, side)
    widen_edges(thin_got, main, nx)
    filter_steps(main, side, diag2, cond2, acc, coef, nx)

    def hop(way, s, p):
        last = s == steps
        here = 0 if s == 1 else 2 * (s - 1) - 1 + way
        slot = 2 * s - 1 if last else 2 * s - 1 + way
        return pltpu.make_async_remote_copy(
            src_ref=cols.at[p, here], dst_ref=cols.at[p, slot], send_sem=z_send.at[way, s - 1, p],
            recv_sem=z_recv.at[way, s - 1, p], device_id=up if way == 0 else down, device_id_type=MESH)

    def hops(s):
        return [(way, p) for p in range(PIECES) for way in range(2)
                if s < steps or p % 2 == way]

    for p in range(PIECES):
        finish(p, acc, unscaled, smooth, cols, nx)
        for way in range(2):
            hop(way, 1, p).start()
    load_rows.wait()
    turn_rows(raw, flat)

    def arrive(s):
        for way, p in hops(s):
            hop(way, s, p).wait_recv()
            if s < steps and (way, p) in hops(s + 1):
                hop(way, s + 1, p).start()

    def block_of(slot):
        s = (slot + 1) // 2
        return lax.rem(me_z + ncr - s, ncr) if slot % 2 else lax.rem(me_z + s, ncr)

    def multiply(first, last):
        count = (last - first) * nc
        depth = cols.shape[-1]
        total = None
        for p in range(PIECES):
            lhs = cols[p, first:last].reshape(count, depth)
            rhs = flat[:, p * depth : (p + 1) * depth]
            part = lax.dot_general(lhs, rhs, (((1,), (1,)), ((), ())), preferred_element_type=jnp.float32)
            total = part if total is None else total + part
        out_a[first:last] = total.astype(jnp.bfloat16).reshape(last - first, nc, flat.shape[0])

    def send_a(slot):
        block = block_of(slot)
        to_low, high = lax.rem(block, low), block // low
        return to_low, high, pltpu.make_async_remote_copy(
            src_ref=out_a.at[slot], dst_ref=in_a.at[high, me_low], send_sem=a_send.at[slot],
            recv_sem=a_recv.at[high, me_low], device_id=(me_high * low + to_low, me_y, me_z), device_id_type=MESH)

    def share(first, last):
        for slot in range(first, last):
            to_low, high, copy = send_a(slot)
            pl.when(to_low != me_low)(copy.start)

            @pl.when(to_low == me_low)
            def _(slot=slot, high=high):
                in_a[high, me_low] = out_a[slot]

    def send_b(h, y):
        return pltpu.make_async_remote_copy(
            src_ref=out_b.at[h, y], dst_ref=in_b.at[me_high * nsy + me_y], send_sem=b_send.at[h, y],
            recv_sem=b_recv.at[me_high * nsy + me_y], device_id=(h * low + me_low, y, me_z), device_id_type=MESH)

    def gather_a(h):
        for q in range(low):
            @pl.when(q != me_low)
            def _(q=q):
                pltpu.make_async_remote_copy(
                    src_ref=out_a.at[0], dst_ref=in_a.at[h, q], send_sem=a_send.at[0],
                    recv_sem=a_recv.at[h, q], device_id=(me_high * low + q, me_y, me_z),
                    device_id_type=MESH).wait_recv()
        total = in_a[h, 0].astype(jnp.float32)
        for q in range(1, low):
            total = total + in_a[h, q].astype(jnp.float32)
        oc = nc // nsy
        for y in range(nsy):
            out_b[h, y] = total[y * oc : (y + 1) * oc]
        for y in range(nsy):
            mine = (h == me_high) & (y == me_y)
            pl.when(jnp.logical_not(mine))(send_b(h, y).start)

            @pl.when(mine)
            def _(y=y):
                in_b[me_high * nsy + me_y] = out_b[h, y]

    early = lax.rem(me_low - me_z + ncr + ncr // 4, ncr) // (ncr // 2 + 1)

    for s in range(1, steps + 1):
        first = 0 if s == 1 else 2 * s - 1
        last = min(2 * s + 1, 2 * steps)
        arrive(s)
        multiply(first, last)
        share(first, last)
        if s == steps - 1:
            gather_a(early)
    gather_a(1 - early)
    for peer in range(2 * nsy):
        h, y = peer // nsy, peer % nsy

        @pl.when((h != me_high) | (y != me_y))
        def _(peer=peer, h=h, y=y):
            pltpu.make_async_remote_copy(
                src_ref=out_b.at[0, 0], dst_ref=in_b.at[peer], send_sem=b_send.at[0, 0],
                recv_sem=b_recv.at[peer], device_id=(h * low + me_low, y, me_z), device_id_type=MESH).wait_recv()
    total = in_b[0]
    for peer in range(1, 2 * nsy):
        total = total + in_b[peer]
    panel_ref[...] = total

    for s in range(1, steps + 1):
        for way, p in hops(s):
            hop(way, s, p).wait_send()
    for slot in range(2 * steps):
        to_low, high, copy = send_a(slot)
        pl.when(to_low != me_low)(copy.wait_send)
    for h in range(2):
        for y in range(nsy):
            pl.when((h != me_high) | (y != me_y))(send_b(h, y).wait_send)


def write_out(smooth, panel, smooth_out, panel_out, sem):
    copies = [
        pltpu.make_async_copy(smooth, smooth_out, sem.at[0]),
        pltpu.make_async_copy(panel, panel_out, sem.at[1]),
    ]
    for copy in copies:
        copy.start()
    for copy in copies:
        copy.wait()


def on_device(sizes, adjoint, sensor_rows, cell_ids, mat_diag, mat_cond, cheb_coef):
    nsx, nsy, ncr = sizes
    nc, nx, ny = adjoint.shape
    nr = sensor_rows.shape[0]
    low = nsx // 2
    wide = nx + 2 * DEG
    oc = nc // nsy
    f32, bf16 = jnp.float32, jnp.bfloat16
    vmem = pl.BlockSpec(memory_space=pltpu.VMEM)
    smem = pl.BlockSpec(memory_space=pltpu.SMEM)
    hbm = pl.BlockSpec(memory_space=pl.ANY)
    dma = pltpu.SemaphoreType.DMA
    smooth, panel = pl.pallas_call(
        functools.partial(kernel, sizes),
        out_shape=(jax.ShapeDtypeStruct((nc * nx, ny), f32), jax.ShapeDtypeStruct((oc, nr), f32)),
        in_specs=[hbm, hbm, vmem, smem, smem, smem],
        out_specs=(vmem, vmem),
        scratch_shapes=[
            pltpu.VMEM((nc * nx, ny), f32),
            pltpu.VMEM((nr, nx, ny), bf16),
            pltpu.VMEM((nr, nx * ny), bf16),
            pltpu.VMEM((3, wide, ny), jnp.int32),
            pltpu.VMEM((2, nx, 8, ny), f32),
            pltpu.VMEM((2, nx, 8, ny), f32),
            pltpu.VMEM((2, wide, 2, 8, ny), f32),
            pltpu.VMEM((2, wide, 8, ny), f32),
            pltpu.VMEM((nx, 2, 8, ny), f32),
            pltpu.VMEM((2, nx // 8, 8, ny), f32),
            pltpu.VMEM((2, wide // 8, 8, ny), f32),
            pltpu.VMEM((2, 8, 16, ny), bf16),
            pltpu.VMEM((2, 8, 16, ny), bf16),
            pltpu.VMEM((3, wide, 8, ny), f32),
            pltpu.VMEM((3, wide, 8, ny), f32),
            pltpu.VMEM((PIECES, ncr, nc, nx * ny // PIECES), bf16),
            pltpu.VMEM((ncr, nc, nr), bf16),
            pltpu.VMEM((2, low, nc, nr), bf16),
            pltpu.VMEM((2, nsy, oc, nr), f32),
            pltpu.VMEM((2 * nsy, oc, nr), f32),
            dma((2,)),
            dma((2, 8)),
            dma((2, 8)),
            dma((2, ncr // 2, PIECES)),
            dma((2, ncr // 2, PIECES)),
            dma((ncr,)),
            dma((2, low)),
            dma((2, nsy)),
            dma((2 * nsy,)),
        ],
        compiler_params=pltpu.CompilerParams(
            collective_id=0, has_side_effects=True, vmem_limit_bytes=62 << 20
        ),
    )(adjoint.reshape(nc * nx, ny), sensor_rows, cell_ids, mat_diag, mat_cond, cheb_coef)
    smooth, panel = pl.pallas_call(
        write_out,
        out_shape=(jax.ShapeDtypeStruct(smooth.shape, f32), jax.ShapeDtypeStruct(panel.shape, f32)),
        in_specs=[vmem, vmem],
        out_specs=(hbm, hbm),
        scratch_shapes=[dma((2,))],
    )(smooth, panel)
    return smooth.reshape(nc, nx, ny), panel.T


def solution(mesh):
    placed = (P("cr", "sx", "sy"), P("cr", "sx", "sy"), P("sx", "sy"), P(), P(), P())
    sizes = tuple(mesh.shape[axis] for axis in ("sx", "sy", "cr"))
    return jax.shard_map(
        functools.partial(on_device, sizes),
        mesh=mesh,
        in_specs=placed,
        out_specs=(P("cr", "sx", "sy"), P("cr", ("sx", "sy"))),
        check_vma=False,
    )
```

```python
import functools

import jax
import jax.numpy as jnp
from jax import lax
from jax.experimental import pallas as pl
from jax.experimental.pallas import tpu as pltpu
from jax.sharding import PartitionSpec as P

DEG = 8
LANES = 128
HALF = LANES // 2
PIECES = 2
MESH = pl.DeviceIdType.MESH


def lane_iota(shape):
    return lax.broadcasted_iota(jnp.int32, shape, len(shape) - 1)


def roll(value, shift):
    return pltpu.roll(value, shift % LANES, value.ndim - 1)


def lookup(ids, table):
    out = jnp.zeros(ids.shape, jnp.float32)
    for material in range(table.shape[0]):
        out = jnp.where(ids == material, table[material], out)
    return out


def load_own(wide, scaled, main, acc, coef):
    nx = scaled.shape[1]
    for x in range(nx):
        for g in range(2):
            value = wide[pl.ds(g * 8 * nx + x, 8, stride=nx), :]
            if g == 1:
                value = roll(value, HALF)
            value = scaled[g, x] * value
            main[0, DEG + x, g] = value
            acc[x, g] = coef[0] * value


def pack_edges(main, packed, nx):
    lane = lane_iota((8, LANES))
    window = lax.rem(lane, HALF) // DEG
    low = lane < HALF
    for xb in range(nx // 8):
        first = jnp.zeros((8, LANES), jnp.float32)
        last = jnp.zeros((8, LANES), jnp.float32)
        for i in range(8):
            m0 = main[0, DEG + 8 * xb + i, 0]
            m1 = main[0, DEG + 8 * xb + i, 1]
            first = jnp.where(window == i, roll(jnp.where(low, m0, m1), 8 * i), first)
            last = jnp.where(window == i, roll(jnp.where(low, m1, m0), 8 * (i + 1)), last)
        packed[0, xb] = first
        packed[1, xb] = last


def thin_edges(main, thin, nx):
    for e, start in enumerate((DEG, nx)):
        for x in range(8):
            thin[e, x] = main[0, start + x].reshape(16, LANES).astype(jnp.bfloat16)


def widen_edges(thin_got, main, nx):
    for e, start in enumerate((0, DEG + nx)):
        for x in range(8):
            main[0, start + x] = thin_got[e, x].astype(jnp.float32).reshape(2, 8, LANES)


def unpack_edges(got, side):
    lane = lax.rem(lane_iota((8, LANES)), HALF)
    for xb in range(got.shape[1]):
        left = got[0, xb]
        right = got[1, xb]
        for i in range(8):
            value = jnp.where(lane >= HALF - DEG, roll(left, -8 * (i + 1)), 0.0)
            side[0, 8 * xb + i] = jnp.where(lane < DEG, roll(right, -8 * i), value)


def build_fields(ids, mat_diag, mat_cond, diag2, cond2):
    middle = ids[1]
    rows = middle.shape[0]
    lane = lane_iota((rows, LANES))
    in_half = lax.rem(lane, HALF)
    lower = lane < HALF
    left = jnp.where(lower, roll(ids[0], HALF), ids[0])
    right = jnp.where(lower, ids[2], roll(ids[2], HALF))
    edges = jnp.where(in_half < DEG, right, jnp.where(in_half >= HALF - DEG, left, -1))
    for t, tile in enumerate((middle, None, edges)):
        if tile is None:
            d, c = roll(diag, HALF), roll(cond, HALF)
        else:
            diag, cond = lookup(tile, mat_diag), lookup(tile, mat_cond)
            d, c = diag, cond
        diag2[t] = jnp.broadcast_to((2.0 * d)[:, None, :], (rows, 8, LANES))
        cond2[t] = jnp.broadcast_to((2.0 * c * c)[:, None, :], (rows, 8, LANES))


def own_cond(ids_ref, mat_cond, scaled, unscaled):
    cond = lookup(ids_ref[...], mat_cond)
    nx = cond.shape[0]
    for g in range(2):
        value = cond if g == 0 else roll(cond, HALF)
        scaled[g] = jnp.broadcast_to(value[:, None, :], (nx, 8, LANES))
        unscaled[g] = jnp.broadcast_to((1.0 / value)[:, None, :], (nx, 8, LANES))


def filter_steps(main, side, diag2, cond2, acc, coef, nx):
    rows = nx + 2 * DEG
    for k in range(1, DEG + 1):
        cur, new = (k + 1) % 2, k % 2
        cuts = [k] + [c for c in range(8, rows, 8) if k < c < rows - k] + [rows - k]
        for a, b in zip(cuts[:-1], cuts[1:]):
            lane = lane_iota((b - a, 8, LANES))
            whole = [main[cur, a - 1 : b + 1, 0], main[cur, a - 1 : b + 1, 1], side[cur, a - 1 : b + 1]]
            middle = [w[1:-1] for w in whole]
            before = [roll(m, 1) for m in middle]
            after = [roll(m, -1) for m in middle]
            wrap_b = (0, HALF)
            wrap_a = (LANES - 1, HALF - 1)
            for t in range(3 if k < DEG else 2):
                if t < 2:
                    lhs = jnp.where(lane == wrap_b[t], before[2], before[t])
                    rhs = jnp.where(lane == wrap_a[t], after[2], after[t])
                else:
                    lhs = jnp.where(lane == wrap_b[0], before[0], jnp.where(lane == wrap_b[1], before[1], before[2]))
                    rhs = jnp.where(lane == wrap_a[0], after[0], jnp.where(lane == wrap_a[1], after[1], after[2]))
                beside = (whole[t][:-2] + whole[t][2:]) + (lhs + rhs)
                value = diag2[t, a:b] * middle[t] + cond2[t, a:b] * beside
                if k == 1:
                    value = 0.5 * value
                elif t < 2:
                    value = value - main[new, a:b, t]
                else:
                    value = value - side[new, a:b]
                if t == 2:
                    side[new, a:b] = value
                else:
                    if k < DEG:
                        main[new, a:b, t] = value
                    if a >= DEG and b <= rows - DEG:
                        acc[a - DEG : b - DEG, t] = acc[a - DEG : b - DEG, t] + coef[k] * value


def finish(acc, unscaled, smooth, cols, nx):
    depth = cols.shape[-1]
    for x in range(nx):
        done = []
        for g in range(2):
            value = acc[x, g] * unscaled[g, x]
            if g == 1:
                value = roll(value, HALF)
            smooth[pl.ds(g * 8 * nx + x, 8, stride=nx), :] = value
            done.append(value)
        at = x * LANES
        cols[at // depth, 0, :, at % depth : at % depth + LANES] = jnp.concatenate(done, axis=0).astype(jnp.bfloat16)


def turn_rows(raw, flat):
    step = 16
    nx = raw.shape[1]

    def body(i, carry):
        at = pl.ds(pl.multiple_of(i * step, step), step)
        turned = jnp.swapaxes(raw[at], 0, 1)
        for x in range(nx):
            flat[at, x * LANES : (x + 1) * LANES] = turned[x]
        return carry

    lax.fori_loop(0, raw.shape[0] // step, body, 0)


def kernel(
    sizes,
    adj_hbm, rows_hbm, ids_ref, mat_diag, mat_cond, coef,
    smooth, panel_ref,
    wide, raw, flat, ids, scaled, unscaled, main, side, acc, packed, got, thin, thin_got, diag2, cond2, cols,
    out_a, in_a, out_b, in_b,
    local_sem, halo_send, halo_recv, z_send, z_recv, a_send, a_recv, b_send, b_recv,
):
    nsx, nsy, ncr = sizes
    low = nsx // 2
    me_x, me_y, me_z = lax.axis_index("sx"), lax.axis_index("sy"), lax.axis_index("cr")
    me_low, me_high = lax.rem(me_x, low), me_x // low
    nx = ids_ref.shape[0]
    nc = out_a.shape[1]
    steps = ncr // 2
    load_adj = pltpu.make_async_copy(adj_hbm, wide, local_sem.at[0])
    load_rows = pltpu.make_async_copy(rows_hbm, raw, local_sem.at[1])
    load_adj.start()
    load_rows.start()

    sides = []
    for dx in (-1, 0, 1):
        for dy in (-1, 0, 1):
            if dx or dy:
                x, y = me_x + dx, me_y + dy
                sides.append((dx, dy, (x >= 0) & (x < nsx) & (y >= 0) & (y < nsy), (x, y, me_z)))
    up = (me_x, me_y, lax.rem(me_z + 1, ncr))
    down = (me_x, me_y, lax.rem(me_z + ncr - 1, ncr))

    barrier = pltpu.get_barrier_semaphore()

    def greet(*device):
        pl.semaphore_signal(barrier, inc=1, device_id=device, device_id_type=MESH)

    greet(*up)
    greet(*down)
    for q in range(low):
        pl.when(q != me_low)(functools.partial(greet, me_high * low + q, me_y, me_z))
    for h in range(2):
        for y in range(nsy):
            pl.when((h != me_high) | (y != me_y))(functools.partial(greet, h * low + me_low, y, me_z))
    for dx in (-1, 1):
        for dy in (-1, 1):
            greet(lax.rem(me_x + nsx + dx, nsx), lax.rem(me_y + nsy + dy, nsy), me_z)
    first_low, last_low = me_low == 0, me_low == low - 1
    pl.when(first_low)(functools.partial(greet, lax.rem(me_x + nsx - 1, nsx), me_y, me_z))
    pl.when(last_low)(functools.partial(greet, lax.rem(me_x + 1, nsx), me_y, me_z))
    peers = 2 + (low - 1) + (2 * nsy - 1) + 4

    own_cond(ids_ref, mat_cond, scaled, unscaled)
    ids[1, DEG : DEG + nx] = ids_ref[...]
    load_adj.wait()
    load_own(wide, scaled, main, acc, coef)
    pack_edges(main, packed, nx)
    thin_edges(main, thin, nx)

    @pl.when(first_low | last_low)
    def _():
        pl.semaphore_wait(barrier, peers + 1)

    @pl.when(jnp.logical_not(first_low | last_low))
    def _():
        pl.semaphore_wait(barrier, peers)

    def rows_from(d):
        return {-1: (0, 8), 0: (0, nx), 1: (nx - 8, nx)}[d]

    def rows_to(d):
        return {-1: (DEG + nx, 2 * DEG + nx), 0: (DEG, DEG + nx), 1: (0, 8)}[d]

    halos = []
    for i, (dx, dy, there, device) in enumerate(sides):
        (a, b), (c, d) = rows_from(dx), rows_to(dx)
        if dy == 0:
            src = thin.at[0 if dx < 0 else 1]
            dst = thin_got.at[1 if dx < 0 else 0]
        else:
            src = packed.at[0 if dy < 0 else 1, a // 8 : b // 8]
            dst = got.at[1 if dy < 0 else 0, c // 8 : d // 8]
        halos.append((there, [
            pltpu.make_async_remote_copy(
                src_ref=src, dst_ref=dst, send_sem=halo_send.at[0, i], recv_sem=halo_recv.at[0, i],
                device_id=device, device_id_type=MESH),
            pltpu.make_async_remote_copy(
                src_ref=ids_ref.at[a:b], dst_ref=ids.at[1 - dy, c:d], send_sem=halo_send.at[1, i],
                recv_sem=halo_recv.at[1, i], device_id=device, device_id_type=MESH),
        ]))

    order = sorted(range(8), key=lambda i: abs(sides[i][1]))
    for i in order:
        there, copies = halos[i]

        @pl.when(there)
        def _(copies=copies):
            copies[0].start()
            copies[1].start()

    for i, (dx, dy, there, device) in enumerate(sides):
        c, d = rows_to(-dx)

        @pl.when(jnp.logical_not(there))
        def _(dx=dx, dy=dy, c=c, d=d):
            ids[1 + dy, c:d] = jnp.full((d - c, LANES), -1, jnp.int32)
            if dy == 0:
                thin_got[0 if dx < 0 else 1] = jnp.zeros((8, 16, LANES), jnp.bfloat16)
            else:
                got[0 if dy < 0 else 1, c // 8 : d // 8] = jnp.zeros(((d - c) // 8, 8, LANES), jnp.float32)

    for i, (dx, dy, there, device) in enumerate(sides):
        there_copies = halos[7 - i][1]

        @pl.when(there)
        def _(mine=halos[i][1], theirs=there_copies):
            for copy in mine:
                copy.wait_send()
            for copy in theirs:
                copy.wait_recv()

    build_fields(ids, mat_diag, mat_cond, diag2, cond2)
    unpack_edges(got, side)
    widen_edges(thin_got, main, nx)
    filter_steps(main, side, diag2, cond2, acc, coef, nx)
    finish(acc, unscaled, smooth, cols, nx)

    def hop(way, s, p):
        last = s == steps
        here = 0 if s == 1 else 2 * (s - 1) - 1 + way
        slot = 2 * s - 1 if last else 2 * s - 1 + way
        return pltpu.make_async_remote_copy(
            src_ref=cols.at[p, here], dst_ref=cols.at[p, slot], send_sem=z_send.at[way, s - 1, p],
            recv_sem=z_recv.at[way, s - 1, p], device_id=up if way == 0 else down, device_id_type=MESH)

    def hops(s):
        return [(way, p) for p in range(PIECES) for way in range(2)
                if s < steps or p % 2 == way]

    for way, p in hops(1):
        hop(way, 1, p).start()
    load_rows.wait()
    turn_rows(raw, flat)

    def arrive(s):
        for way, p in hops(s):
            hop(way, s, p).wait_recv()
            if s < steps and (way, p) in hops(s + 1):
                hop(way, s + 1, p).start()

    def block_of(slot):
        s = (slot + 1) // 2
        return lax.rem(me_z + ncr - s, ncr) if slot % 2 else lax.rem(me_z + s, ncr)

    def multiply(first, last, at=slice(None)):
        count = (last - first) * nc
        depth = cols.shape[-1]
        total = None
        for p in range(PIECES):
            lhs = cols[p, first:last].reshape(count, depth)
            rhs = flat[at, p * depth : (p + 1) * depth]
            part = lax.dot_general(lhs, rhs, (((1,), (1,)), ((), ())), preferred_element_type=jnp.float32)
            total = part if total is None else total + part
        out_a[first:last, :, at] = total.astype(jnp.bfloat16).reshape(last - first, nc, total.shape[1])

    def send_a(slot, at=slice(None)):
        block = block_of(slot)
        to_low, high = lax.rem(block, low), block // low
        return to_low, high, pltpu.make_async_remote_copy(
            src_ref=out_a.at[slot, :, at], dst_ref=in_a.at[high, me_low, :, at], send_sem=a_send.at[slot],
            recv_sem=a_recv.at[high, me_low], device_id=(me_high * low + to_low, me_y, me_z), device_id_type=MESH)

    def share(first, last, at=slice(None)):
        for slot in range(first, last):
            to_low, high, copy = send_a(slot, at)
            pl.when(to_low != me_low)(copy.start)

            @pl.when(to_low == me_low)
            def _(slot=slot, high=high):
                in_a[high, me_low, :, at] = out_a[slot, :, at]

    def send_b(h, y):
        return pltpu.make_async_remote_copy(
            src_ref=out_b.at[h, y], dst_ref=in_b.at[me_high * nsy + me_y], send_sem=b_send.at[h, y],
            recv_sem=b_recv.at[me_high * nsy + me_y], device_id=(h * low + me_low, y, me_z), device_id_type=MESH)

    def gather_a(h):
        for q in range(low):
            @pl.when(q != me_low)
            def _(q=q):
                pltpu.make_async_remote_copy(
                    src_ref=out_a.at[0], dst_ref=in_a.at[h, q], send_sem=a_send.at[0],
                    recv_sem=a_recv.at[h, q], device_id=(me_high * low + q, me_y, me_z),
                    device_id_type=MESH).wait_recv()
        total = in_a[h, 0].astype(jnp.float32)
        for q in range(1, low):
            total = total + in_a[h, q].astype(jnp.float32)
        oc = nc // nsy
        for y in range(nsy):
            out_b[h, y] = total[y * oc : (y + 1) * oc]
        for y in range(nsy):
            mine = (h == me_high) & (y == me_y)
            pl.when(jnp.logical_not(mine))(send_b(h, y).start)

            @pl.when(mine)
            def _(y=y):
                in_b[me_high * nsy + me_y] = out_b[h, y]

    early = lax.rem(me_low - me_z + ncr + ncr // 4, ncr) // (ncr // 2 + 1)

    for s in range(1, steps + 1):
        first = 0 if s == 1 else 2 * s - 1
        last = min(2 * s + 1, 2 * steps)
        arrive(s)
        if s < steps:
            multiply(first, last)
            share(first, last)
        else:
            for start in range(0, flat.shape[0], 256):
                at = slice(start, min(start + 256, flat.shape[0]))
                multiply(first, last, at)
                share(first, last, at)
        if s == steps - 1:
            gather_a(early)
    gather_a(1 - early)
    for peer in range(2 * nsy):
        h, y = peer // nsy, peer % nsy

        @pl.when((h != me_high) | (y != me_y))
        def _(peer=peer, h=h, y=y):
            pltpu.make_async_remote_copy(
                src_ref=out_b.at[0, 0], dst_ref=in_b.at[peer], send_sem=b_send.at[0, 0],
                recv_sem=b_recv.at[peer], device_id=(h * low + me_low, y, me_z), device_id_type=MESH).wait_recv()
    total = in_b[0]
    for peer in range(1, 2 * nsy):
        total = total + in_b[peer]
    panel_ref[...] = total

    for s in range(1, steps + 1):
        for way, p in hops(s):
            hop(way, s, p).wait_send()
    for slot in range(2 * steps):
        to_low, high, copy = send_a(slot)
        pl.when(to_low != me_low)(copy.wait_send)
    for h in range(2):
        for y in range(nsy):
            pl.when((h != me_high) | (y != me_y))(send_b(h, y).wait_send)


def write_out(smooth, panel, smooth_out, panel_out, sem):
    copies = [
        pltpu.make_async_copy(smooth, smooth_out, sem.at[0]),
        pltpu.make_async_copy(panel, panel_out, sem.at[1]),
    ]
    for copy in copies:
        copy.start()
    for copy in copies:
        copy.wait()


def on_device(sizes, adjoint, sensor_rows, cell_ids, mat_diag, mat_cond, cheb_coef):
    nsx, nsy, ncr = sizes
    nc, nx, ny = adjoint.shape
    nr = sensor_rows.shape[0]
    low = nsx // 2
    wide = nx + 2 * DEG
    oc = nc // nsy
    f32, bf16 = jnp.float32, jnp.bfloat16
    vmem = pl.BlockSpec(memory_space=pltpu.VMEM)
    smem = pl.BlockSpec(memory_space=pltpu.SMEM)
    hbm = pl.BlockSpec(memory_space=pl.ANY)
    dma = pltpu.SemaphoreType.DMA
    smooth, panel = pl.pallas_call(
        functools.partial(kernel, sizes),
        out_shape=(jax.ShapeDtypeStruct((nc * nx, ny), f32), jax.ShapeDtypeStruct((oc, nr), f32)),
        in_specs=[hbm, hbm, vmem, smem, smem, smem],
        out_specs=(vmem, vmem),
        scratch_shapes=[
            pltpu.VMEM((nc * nx, ny), f32),
            pltpu.VMEM((nr, nx, ny), bf16),
            pltpu.VMEM((nr, nx * ny), bf16),
            pltpu.VMEM((3, wide, ny), jnp.int32),
            pltpu.VMEM((2, nx, 8, ny), f32),
            pltpu.VMEM((2, nx, 8, ny), f32),
            pltpu.VMEM((2, wide, 2, 8, ny), f32),
            pltpu.VMEM((2, wide, 8, ny), f32),
            pltpu.VMEM((nx, 2, 8, ny), f32),
            pltpu.VMEM((2, nx // 8, 8, ny), f32),
            pltpu.VMEM((2, wide // 8, 8, ny), f32),
            pltpu.VMEM((2, 8, 16, ny), bf16),
            pltpu.VMEM((2, 8, 16, ny), bf16),
            pltpu.VMEM((3, wide, 8, ny), f32),
            pltpu.VMEM((3, wide, 8, ny), f32),
            pltpu.VMEM((PIECES, ncr, nc, nx * ny // PIECES), bf16),
            pltpu.VMEM((ncr, nc, nr), bf16),
            pltpu.VMEM((2, low, nc, nr), bf16),
            pltpu.VMEM((2, nsy, oc, nr), f32),
            pltpu.VMEM((2 * nsy, oc, nr), f32),
            dma((2,)),
            dma((2, 8)),
            dma((2, 8)),
            dma((2, ncr // 2, PIECES)),
            dma((2, ncr // 2, PIECES)),
            dma((ncr,)),
            dma((2, low)),
            dma((2, nsy)),
            dma((2 * nsy,)),
        ],
        compiler_params=pltpu.CompilerParams(
            collective_id=0, has_side_effects=True, vmem_limit_bytes=62 << 20
        ),
    )(adjoint.reshape(nc * nx, ny), sensor_rows, cell_ids, mat_diag, mat_cond, cheb_coef)
    smooth, panel = pl.pallas_call(
        write_out,
        out_shape=(jax.ShapeDtypeStruct(smooth.shape, f32), jax.ShapeDtypeStruct(panel.shape, f32)),
        in_specs=[vmem, vmem],
        out_specs=(hbm, hbm),
        scratch_shapes=[dma((2,))],
    )(smooth, panel)
    return smooth.reshape(nc, nx, ny), panel.T


def solution(mesh):
    placed = (P("cr", "sx", "sy"), P("cr", "sx", "sy"), P("sx", "sy"), P(), P(), P())
    sizes = tuple(mesh.shape[axis] for axis in ("sx", "sy", "cr"))
    return jax.shard_map(
        functools.partial(on_device, sizes),
        mesh=mesh,
        in_specs=placed,
        out_specs=(P("cr", "sx", "sy"), P("cr", ("sx", "sy"))),
        check_vma=False,
    )
```
